32 devices in a mesh: group: 16 (over z, y, core), tensor: 2 (over x).
Axes of the slice: x: 2, y: 2, z: 4, core: 2. Of those that a mesh axis runs over, the one named last changes fastest.
Arguments:
- turns: bfloat16 [16, 256, 4096], P('group', 'tensor'), may hold values from -16 to 16
- query_store: bfloat16 [16, 256, 4096], P('group', None, 'tensor'), may hold values from -0.09375 to 0.09375
- key_block_holder: bfloat16 [16, 256, 4, 128], P('group'), may hold values from -0.09375 to 0.09375
- value_block_holder: bfloat16 [16, 256, 4, 128], P('group'), may hold values from -0.09375 to 0.09375
- query_bias: float32 [4096], P('tensor'), may hold values from -3 to 3
- key_projection_bias: float32 [512], replicated, may hold values from -3 to 3
- value_projection_bias: float32 [512], replicated, may hold values from -3 to 3
- owner: int32 [16], replicated, may hold values from 0 to 15, each once
- lengths: int32 [16], P('group'), may hold values from 1 to 256, as said below
Outputs:
- attended: bfloat16 [16, 256, 4096], P('group', None, 'tensor')
The draws below stay inside these ranges and needn't reach their ends.
Inputs may be any that keep to these rules, and one draw needn't show every extreme that they name: `owner`: each group index holds exactly one block. `lengths`: some group's turn fills all 256 positions.
All inputs are finite; a program needn't handle non-finite values.
Results may differ from the reference program's by a relative error of at most 0.0055.
The reference program's roundings to bfloat16 on the way (of `weights`) count: a program that leaves them out, or rounds other values in their place, can miss the bound.
Values may be sent and summed in bfloat16 or wider, within the bound.
A program may use at most 128 MiB of HBM per device.

```python
import jax
import jax.numpy as jnp
from jax import lax

INPUT_FEATURES = 4096
QUERY_HEADS = 32
KEY_VALUE_HEADS = 4
HEAD_SIZE = 128
ROLLOUT_GROUPS = 16
TURN_TOKENS = 256
OWNED_BLOCK_ROWS = 256


def draw_turns(key, part):
    return jnp.clip(jax.random.normal(key, (ROLLOUT_GROUPS, TURN_TOKENS, INPUT_FEATURES), jnp.float32), -4.0, 4.0).astype(jnp.bfloat16)


def draw_lengths(key, part):
    first, second = jax.random.split(jax.random.fold_in(key, 7))
    values = jax.random.randint(first, (ROLLOUT_GROUPS,), 1, TURN_TOKENS + 1)
    full_at = jax.random.randint(second, (), 0, ROLLOUT_GROUPS)
    return values.at[full_at].set(TURN_TOKENS).astype(jnp.int32)


def shard_levels(stream_key, shape, shards, low, top_value):
    level, own = 1.0, jax.random.fold_in(stream_key, 6)
    for axis_at, blocks in shards:
        heights = jnp.exp(jax.random.uniform(jax.random.fold_in(own, axis_at), (blocks,), jnp.float32, low / len(shards), top_value / len(shards)))
        level = level * jnp.repeat(heights, shape[axis_at] // blocks).reshape([-1 if axis == axis_at else 1 for axis in range(len(shape))])
    return level


def scatter_about(own_key, extent, width, limit, pieces=(), kind=jnp.bfloat16):
    entries = width * jax.random.normal(own_key, extent, jnp.float32)
    if pieces:
        entries = entries * shard_levels(own_key, extent, pieces, -0.22, 0.18)
    return jnp.clip(entries, -limit, limit).astype(kind)


def setup_inputs(seed: int = 0) -> dict:
    key_list = jax.random.split(jax.random.key(seed), 10)
    turns = draw_turns(jax.random.fold_in(key_list[9], 71), 0)
    query_store = scatter_about(key_list[1], (ROLLOUT_GROUPS, OWNED_BLOCK_ROWS, QUERY_HEADS * HEAD_SIZE), INPUT_FEATURES ** -0.5, 0.09375, ((0, 16), (2, 2)))
    key_block_holder = scatter_about(key_list[2], (ROLLOUT_GROUPS, OWNED_BLOCK_ROWS, KEY_VALUE_HEADS, HEAD_SIZE), INPUT_FEATURES ** -0.5, 0.09375, ((0, 16),))
    value_block_holder = scatter_about(key_list[3], (ROLLOUT_GROUPS, OWNED_BLOCK_ROWS, KEY_VALUE_HEADS, HEAD_SIZE), INPUT_FEATURES ** -0.5, 0.09375, ((0, 16),))
    query_bias = scatter_about(key_list[4], (QUERY_HEADS * HEAD_SIZE,), 0.5, 3.0, ((0, 2),), jnp.float32)
    key_projection_bias = scatter_about(key_list[5], (KEY_VALUE_HEADS * HEAD_SIZE,), 0.5, 3.0, (), jnp.float32)
    value_projection_bias = scatter_about(key_list[6], (KEY_VALUE_HEADS * HEAD_SIZE,), 0.5, 3.0, (), jnp.float32)
    owner = jax.random.permutation(key_list[7], ROLLOUT_GROUPS).astype(jnp.int32)
    lengths = draw_lengths(jax.random.fold_in(key_list[9], 71), 0)
    return {"turns": turns, "query_store": query_store, "key_block_holder": key_block_holder, "value_block_holder": value_block_holder, "query_bias": query_bias, "key_projection_bias": key_projection_bias, "value_projection_bias": value_projection_bias, "owner": owner, "lengths": lengths}


rotary_base = 1000000.0


def rotary(heads, positions):
    half = heads.shape[-1] // 2
    expo = jnp.arange(half, dtype=jnp.float32) * 2.0 / heads.shape[-1]
    freqs = rotary_base ** (-expo)
    angles = positions[:, None] * freqs[None, :]
    cosine = jnp.cos(angles)[None]
    sine = jnp.sin(angles)[None]
    first = heads[..., :half]
    second = heads[..., half:]
    return jnp.concatenate([first * cosine - second * sine, second * cosine + first * sine], axis=-1)


def reference(turns, query_store, key_block_holder, value_block_holder, query_bias, key_projection_bias, value_projection_bias, owner, lengths):
    w_query = query_store[owner].reshape(INPUT_FEATURES, QUERY_HEADS * HEAD_SIZE)
    key_weight_matrix = key_block_holder[owner].reshape(INPUT_FEATURES, KEY_VALUE_HEADS * HEAD_SIZE)
    value_weight_matrix = value_block_holder[owner].reshape(INPUT_FEATURES, KEY_VALUE_HEADS * HEAD_SIZE)
    query_per_key_head = QUERY_HEADS // KEY_VALUE_HEADS
    positions = jnp.arange(TURN_TOKENS, dtype=jnp.float32)
    index = jnp.arange(TURN_TOKENS, dtype=jnp.int32)
    causal = index[None, :] <= index[:, None]

    def one_group(inputs):
        hidden, length = inputs
        raw_query = jnp.dot(hidden, w_query, preferred_element_type=jnp.float32) + query_bias
        unbiased_key = jnp.dot(hidden, key_weight_matrix, preferred_element_type=jnp.float32) + key_projection_bias
        unbiased_value = jnp.dot(hidden, value_weight_matrix, preferred_element_type=jnp.float32) + value_projection_bias
        raw_query = raw_query.reshape(TURN_TOKENS, QUERY_HEADS, HEAD_SIZE).transpose(1, 0, 2)
        unbiased_key = unbiased_key.reshape(TURN_TOKENS, KEY_VALUE_HEADS, HEAD_SIZE).transpose(1, 0, 2)
        unbiased_value = unbiased_value.reshape(TURN_TOKENS, KEY_VALUE_HEADS, HEAD_SIZE).transpose(1, 0, 2)
        query = rotary(raw_query, positions).astype(jnp.bfloat16)
        key = rotary(unbiased_key, positions).astype(jnp.bfloat16)
        value = unbiased_value.astype(jnp.bfloat16)
        key_full = jnp.repeat(key, query_per_key_head, axis=0).astype(jnp.float32)
        value_full = jnp.repeat(value, query_per_key_head, axis=0).astype(jnp.float32)
        scores = jnp.einsum("htd,hsd->hts", query.astype(jnp.float32), key_full) * (HEAD_SIZE ** -0.5)
        scores = jnp.where(causal[None], scores, -jnp.inf)
        top = jnp.max(scores, axis=-1, keepdims=True)
        expd = jnp.exp(scores - top)
        weights = (expd / jnp.sum(expd, axis=-1, keepdims=True)).astype(jnp.bfloat16)
        mixed = jnp.einsum("hts,hsd->htd", weights.astype(jnp.float32), value_full)
        mixed = mixed.transpose(1, 0, 2).reshape(TURN_TOKENS, QUERY_HEADS * HEAD_SIZE)
        live = (index < length)[:, None]
        return jnp.where(live, mixed, 0.0).astype(jnp.bfloat16)

    return lax.map(one_group, (turns, lengths))
```

```python
import jax
import jax.numpy as jnp
import numpy as np
from jax import lax
from jax.experimental import pallas as pl
from jax.experimental.pallas import tpu as pltpu
from jax.sharding import PartitionSpec as P

QUERY_HEADS = 32
KEY_VALUE_HEADS = 4
HEAD_SIZE = 128


rotary_base = 1000000.0


def rotary(heads, positions):
    half = heads.shape[-1] // 2
    expo = jnp.arange(half, dtype=jnp.float32) * 2.0 / heads.shape[-1]
    freqs = rotary_base ** (-expo)
    angles = positions[:, None] * freqs[None, :]
    cosine = jnp.cos(angles)[None]
    sine = jnp.sin(angles)[None]
    first = heads[..., :half]
    second = heads[..., half:]
    return jnp.concatenate(
        [first * cosine - second * sine, second * cosine + first * sine], axis=-1
    )


def per_device(
    turns,
    query_store,
    key_block_holder,
    value_block_holder,
    query_bias,
    key_projection_bias,
    value_projection_bias,
    owner,
    lengths,
):
    tensor_index = lax.axis_index("tensor")
    group_count = lax.axis_size("group")
    gathered = lax.all_gather(turns, "tensor", axis=1, tiled=True)[0]
    token_count = gathered.shape[0]
    block_rows = query_store.shape[1]
    query_cols = query_store.shape[2]
    heads_dev = query_cols // HEAD_SIZE
    query_per_key_head = QUERY_HEADS // KEY_VALUE_HEADS
    key_value_per_group = max(1, heads_dev // query_per_key_head)
    key_value_leading = tensor_index * heads_dev // query_per_key_head
    keys_mine = lax.dynamic_slice_in_dim(
        key_block_holder, key_value_leading, key_value_per_group, 2
    ).reshape(1, block_rows, key_value_per_group * HEAD_SIZE)
    values_mine = lax.dynamic_slice_in_dim(
        value_block_holder, key_value_leading, key_value_per_group, 2
    ).reshape(1, block_rows, key_value_per_group * HEAD_SIZE)
    inverse = (
        jnp.zeros((group_count,), jnp.int32).at[owner].set(jnp.arange(group_count, dtype=jnp.int32))
    )
    ordered = jnp.stack(
        [
            lax.dynamic_slice_in_dim(gathered, inverse[holder] * block_rows, block_rows, 1)
            for holder in range(group_count)
        ],
        axis=1,
    )
    proj_query = jnp.einsum(
        "tgc,gcn->tn",
        ordered,
        lax.all_gather(query_store, "group", axis=0, tiled=True),
        preferred_element_type=jnp.float32,
    )
    proj_key = jnp.einsum(
        "tgc,gcn->tn",
        ordered,
        lax.all_gather(keys_mine, "group", axis=0, tiled=True),
        preferred_element_type=jnp.float32,
    )
    proj_value = jnp.einsum(
        "tgc,gcn->tn",
        ordered,
        lax.all_gather(values_mine, "group", axis=0, tiled=True),
        preferred_element_type=jnp.float32,
    )
    key_bias_rows = lax.dynamic_slice_in_dim(
        key_projection_bias.reshape(KEY_VALUE_HEADS, HEAD_SIZE),
        key_value_leading,
        key_value_per_group,
        0,
    ).reshape(key_value_per_group * HEAD_SIZE)
    bias_values = lax.dynamic_slice_in_dim(
        value_projection_bias.reshape(KEY_VALUE_HEADS, HEAD_SIZE),
        key_value_leading,
        key_value_per_group,
        0,
    ).reshape(key_value_per_group * HEAD_SIZE)
    positions = jnp.arange(token_count, dtype=jnp.float32)
    raw_query = (
        (proj_query + query_bias).reshape(token_count, heads_dev, HEAD_SIZE).transpose(1, 0, 2)
    )
    unbiased_key = (
        (proj_key + key_bias_rows)
        .reshape(token_count, key_value_per_group, HEAD_SIZE)
        .transpose(1, 0, 2)
    )
    unbiased_value = (
        (proj_value + bias_values)
        .reshape(token_count, key_value_per_group, HEAD_SIZE)
        .transpose(1, 0, 2)
    )
    queries = rotary(raw_query, positions).astype(jnp.bfloat16)
    keys_rot = rotary(unbiased_key, positions).astype(jnp.bfloat16)
    values_cast = unbiased_value.astype(jnp.bfloat16)
    repeat_count = heads_dev // key_value_per_group
    keys_full = jnp.repeat(keys_rot, repeat_count, axis=0)
    values_full = jnp.repeat(values_cast, repeat_count, axis=0)
    index = jnp.arange(token_count, dtype=jnp.int32)
    span = min(256, token_count)
    outputs = []
    for block in range(token_count // span):
        first = block * span
        last = first + span
        scores = jnp.einsum(
            "htd,hsd->hts",
            queries[:, first:last],
            keys_full[:, :last],
            preferred_element_type=jnp.float32,
        ) * HEAD_SIZE ** (-0.5)
        causal = index[None, :last] <= index[first:last, None]
        scores = jnp.where(causal[None], scores, -jnp.inf)
        top = jnp.max(scores, axis=-1, keepdims=True)
        expd = jnp.exp(scores - top)
        weights = (expd / jnp.sum(expd, axis=-1, keepdims=True)).astype(jnp.bfloat16)
        outputs.append(
            jnp.einsum(
                "hts,hsd->htd", weights, values_full[:, :last], preferred_element_type=jnp.float32
            )
        )
    mixed = jnp.concatenate(outputs, axis=1)
    mixed = mixed.transpose(1, 0, 2).reshape(token_count, query_cols)
    live = (index < lengths[0])[:, None]
    return jnp.where(live, mixed, 0.0).astype(jnp.bfloat16)[None]


RING = 8
BLOCKS = 16
ROWS = 256
TOKENS = 256
WIDTH_A = 768
WIDTH_B = 512
MESH = pl.DeviceIdType.MESH


def group_of(place, core):
    y = place // 4
    z = place + y * (7 - 2 * place)
    return z * 4 + y * 2 + core


def ring_kernel(
    row_block_ref,
    length_ref,
    turns_ref,
    store_ref,
    kv_ref,
    query_bias_ref,
    key_bias_ref,
    value_bias_ref,
    cosine_ref,
    sine_ref,
    out_ref,
    x_ref,
    wa_ref,
    wb_ref,
    acca_ref,
    accb_ref,
    keys_ref,
    values_ref,
    local_sem,
    x_local,
    x_send,
    x_recv,
    ring_send,
    ring_recv,
    sib_send,
    sib_recv,
):
    g = lax.axis_index("group")
    t = lax.axis_index("tensor")
    core = lax.rem(g, 2)
    y = lax.rem(g // 2, 2)
    z = g // 4
    r = z + y * (7 - 2 * z)
    other = 1 - core
    onward = (group_of(lax.rem(r + 1, RING), core), group_of(lax.rem(r + RING - 1, RING), core))
    sibling = g + 1 - 2 * core
    half = TOKENS // 2
    weights = (wa_ref, wb_ref)
    accs = (acca_ref, accb_ref)

    mine = pl.ds(pl.multiple_of(t * half, half), half)
    x_loads = [
        pltpu.make_async_copy(
            turns_ref.at[0, :, b * ROWS : b * ROWS + ROWS], x_ref.at[b, mine], x_local.at[b]
        )
        for b in range(BLOCKS)
    ]
    loads = []
    for d in range(2):
        loads.append(
            pltpu.make_async_copy(
                kv_ref.at[:, d * 256 : d * 256 + 256],
                wa_ref.at[core, r, d, :, 0:256],
                local_sem.at[3 * d],
            )
        )
        loads.append(
            pltpu.make_async_copy(
                store_ref.at[0, :, d * 1024 : d * 1024 + 512],
                wa_ref.at[core, r, d, :, 256:768],
                local_sem.at[1 + 3 * d],
            )
        )
        loads.append(
            pltpu.make_async_copy(
                store_ref.at[0, :, d * 1024 + 512 : d * 1024 + 1024],
                wb_ref.at[core, r, d],
                local_sem.at[2 + 3 * d],
            )
        )
    for load in loads + x_loads:
        load.start()

    barrier = pltpu.get_barrier_semaphore()
    for partner in ((onward[0], t), (onward[1], t), (sibling, t), (g, 1 - t)):
        pl.semaphore_signal(barrier, inc=1, device_id=partner, device_id_type=MESH)
    pl.semaphore_wait(barrier, 4)

    def came_from(d, j):
        return lax.rem(r + RING - j, RING) if d == 0 else lax.rem(r + j, RING)

    def ring_copy(d, u, s):
        slot = weights[u].at[core, came_from(d, s), d]
        return pltpu.make_async_remote_copy(
            src_ref=slot,
            dst_ref=slot,
            send_sem=ring_send.at[d, u, s],
            recv_sem=ring_recv.at[d, u, s],
            device_id=(onward[d], t),
            device_id_type=MESH,
        )

    def ring_arrival(d, u, s):
        slot = weights[u].at[core, came_from(d, s + 1), d]
        return pltpu.make_async_remote_copy(
            src_ref=slot,
            dst_ref=slot,
            send_sem=ring_send.at[d, u, s],
            recv_sem=ring_recv.at[d, u, s],
            device_id=(onward[d], t),
            device_id_type=MESH,
        )

    def sib_copy(d, u, j):
        slot = weights[u].at[core, came_from(d, j), d]
        return pltpu.make_async_remote_copy(
            src_ref=slot,
            dst_ref=slot,
            send_sem=sib_send.at[d, u, j],
            recv_sem=sib_recv.at[d, u, j],
            device_id=(sibling, t),
            device_id_type=MESH,
        )

    def sib_arrival(d, u, j):
        slot = weights[u].at[other, came_from(d, j), d]
        return pltpu.make_async_remote_copy(
            src_ref=slot,
            dst_ref=slot,
            send_sem=sib_send.at[d, u, j],
            recv_sem=sib_recv.at[d, u, j],
            device_id=(sibling, t),
            device_id_type=MESH,
        )

    x_copy = pltpu.make_async_remote_copy(
        src_ref=x_ref.at[:, mine],
        dst_ref=x_ref.at[:, mine],
        send_sem=x_send,
        recv_sem=x_recv,
        device_id=(g, 1 - t),
        device_id_type=MESH,
    )

    for load in loads:
        load.wait()
    for u in range(2):
        for d in range(2):
            ring_copy(d, u, 0).start()
    for load in x_loads:
        load.wait()
    x_copy.start()
    for u in range(2):
        for d in range(2):
            sib_copy(d, u, 0).start()

    for d in range(2):
        head = pl.ds(pl.multiple_of((2 * t + d) * HEAD_SIZE, HEAD_SIZE), HEAD_SIZE)
        acca_ref[d, :, 0:128] = jnp.broadcast_to(key_bias_ref[:, head], (TOKENS, 128))
        acca_ref[d, :, 128:256] = jnp.broadcast_to(value_bias_ref[:, head], (TOKENS, 128))
        acca_ref[d, :, 256:768] = jnp.broadcast_to(
            query_bias_ref[:, d * 1024 : d * 1024 + 512], (TOKENS, 512)
        )
        accb_ref[d] = jnp.broadcast_to(
            query_bias_ref[:, d * 1024 + 512 : d * 1024 + 1024], (TOKENS, 512)
        )

    def add_product(u, d, place, which):
        holder = group_of(place, which)
        block = x_ref[row_block_ref[holder]]
        accs[u][d] += jnp.dot(
            block, weights[u][which, place, d], preferred_element_type=jnp.float32
        )

    def use_own(j):
        for u in range(2):
            for d in range(2):
                add_product(u, d, came_from(d, j), core)

    def use_sibling(j):
        for u in range(2):
            for d in range(2):
                sib_arrival(d, u, j).wait_recv()
                add_product(u, d, came_from(d, j), other)

    def step(s, carry):
        for u in range(2):
            for d in range(2):
                ring_arrival(d, u, s).wait_recv()

                @pl.when(s < RING - 2)
                def _():
                    ring_copy(d, u, s + 1).start()

                sib_copy(d, u, s + 1).start()

        @pl.when(s == 0)
        def _():
            x_copy.wait_recv()

        use_own(s)
        use_sibling(s)
        return carry

    lax.fori_loop(0, RING - 1, step, 0)
    use_own(RING - 1)
    use_sibling(RING - 1)

    def rotate(raw):
        return (raw * cosine_ref[...] + pltpu.roll(raw, 64, 1) * sine_ref[...]).astype(jnp.bfloat16)

    for d in range(2):
        keys_ref[d] = rotate(acca_ref[d, :, 0:128])
        values_ref[d] = acca_ref[d, :, 128:256].astype(jnp.bfloat16)

    length = length_ref[0]
    scale = HEAD_SIZE ** (-0.5)

    def attend(raw, d):
        query = rotate(raw)
        parts = []
        for piece in range(2):
            low, high = piece * half, piece * half + half
            scores = (
                lax.dot_general(
                    query[low:high],
                    keys_ref[d, 0:high],
                    (((1,), (1,)), ((), ())),
                    preferred_element_type=jnp.float32,
                )
                * scale
            )
            rows = lax.broadcasted_iota(jnp.int32, (half, high), 0) + low
            cols = lax.broadcasted_iota(jnp.int32, (half, high), 1)
            scores = jnp.where(cols <= rows, scores, -jnp.inf)
            top = jnp.max(scores, axis=-1, keepdims=True)
            expd = jnp.exp(scores - top)
            total = jnp.sum(expd, axis=-1, keepdims=True)
            shares = (expd / total).astype(jnp.bfloat16)
            mixed = jnp.dot(shares, values_ref[d, 0:high], preferred_element_type=jnp.float32)
            live = lax.broadcasted_iota(jnp.int32, (half, HEAD_SIZE), 0) + low < length
            parts.append(jnp.where(live, mixed, 0.0).astype(jnp.bfloat16))
        return parts

    def head_step(h, carry):
        lane = pl.multiple_of(h * HEAD_SIZE, HEAD_SIZE)
        for d in range(2):
            for u in range(2):
                start = 256 if u == 0 else 0
                raw = accs[u][d, :, pl.ds(start + lane, HEAD_SIZE)]
                to = pl.ds(d * 1024 + u * 512 + lane, HEAD_SIZE)
                parts = attend(raw, d)
                for piece in range(2):
                    out_ref[0, piece * half : piece * half + half, to] = parts[piece]
        return carry

    lax.fori_loop(0, 4, head_step, 0)

    x_copy.wait_send()

    def drain(s, carry):
        for u in range(2):
            for d in range(2):
                ring_copy(d, u, s).wait_send()
                sib_copy(d, u, s).wait_send()
        return carry

    lax.fori_loop(0, RING - 1, drain, 0)
    for u in range(2):
        for d in range(2):
            sib_copy(d, u, RING - 1).wait_send()


def rotary_tables():
    freqs = rotary_base ** (-2.0 * np.arange(64) / HEAD_SIZE)
    angles = np.arange(TOKENS)[:, None] * freqs[None, :]
    cosine, sine = np.cos(angles), np.sin(angles)
    return (
        np.concatenate([cosine, cosine], axis=1).astype(np.float32),
        np.concatenate([-sine, sine], axis=1).astype(np.float32),
    )


def per_device_ring(
    turns,
    query_store,
    key_block_holder,
    value_block_holder,
    query_bias,
    key_projection_bias,
    value_projection_bias,
    owner,
    lengths,
):
    t = lax.axis_index("tensor")
    keys_mine = lax.dynamic_slice_in_dim(key_block_holder[0], 2 * t, 2, 1)
    values_mine = lax.dynamic_slice_in_dim(value_block_holder[0], 2 * t, 2, 1)
    kv = jnp.concatenate([keys_mine, values_mine], axis=2).reshape(ROWS, 512)
    numbers = jnp.arange(BLOCKS, dtype=jnp.int32)
    row_block = jnp.sum(
        jnp.where(owner[None, :] == numbers[:, None], numbers[None, :], 0), axis=1, dtype=jnp.int32
    )
    cosine, sine = rotary_tables()
    smem = pl.BlockSpec(memory_space=pltpu.SMEM)
    vmem = pl.BlockSpec(memory_space=pltpu.VMEM)
    hbm = pl.BlockSpec(memory_space=pl.ANY)
    return pl.pallas_call(
        ring_kernel,
        out_shape=jax.ShapeDtypeStruct((1, TOKENS, 2048), jnp.bfloat16),
        in_specs=[smem, smem, hbm, hbm, hbm, vmem, vmem, vmem, vmem, vmem],
        out_specs=vmem,
        scratch_shapes=[
            pltpu.VMEM((BLOCKS, TOKENS, ROWS), jnp.bfloat16),
            pltpu.VMEM((2, RING, 2, ROWS, WIDTH_A), jnp.bfloat16),
            pltpu.VMEM((2, RING, 2, ROWS, WIDTH_B), jnp.bfloat16),
            pltpu.VMEM((2, TOKENS, WIDTH_A), jnp.float32),
            pltpu.VMEM((2, TOKENS, WIDTH_B), jnp.float32),
            pltpu.VMEM((2, TOKENS, HEAD_SIZE), jnp.bfloat16),
            pltpu.VMEM((2, TOKENS, HEAD_SIZE), jnp.bfloat16),
            pltpu.SemaphoreType.DMA((6,)),
            pltpu.SemaphoreType.DMA((BLOCKS,)),
            pltpu.SemaphoreType.DMA,
            pltpu.SemaphoreType.DMA,
            pltpu.SemaphoreType.DMA((2, 2, RING - 1)),
            pltpu.SemaphoreType.DMA((2, 2, RING - 1)),
            pltpu.SemaphoreType.DMA((2, 2, RING)),
            pltpu.SemaphoreType.DMA((2, 2, RING)),
        ],
        compiler_params=pltpu.CompilerParams(
            collective_id=0, has_side_effects=True, vmem_limit_bytes=48 * 1024 * 1024
        ),
    )(
        row_block,
        lengths,
        turns,
        query_store,
        kv,
        query_bias[None],
        key_projection_bias[None],
        value_projection_bias[None],
        jnp.asarray(cosine),
        jnp.asarray(sine),
    )


def pick(turns, *rest):
    fits = lax.axis_size("group") == 16 and lax.axis_size("tensor") == 2
    fits = fits and turns.shape[1:] == (128, 4096)
    return per_device_ring(turns, *rest) if fits else per_device(turns, *rest)


def solution(mesh):
    in_specs = (
        P("group", "tensor", None),
        P("group", None, "tensor"),
        P("group", None, None, None),
        P("group", None, None, None),
        P("tensor"),
        P(),
        P(),
        P(),
        P("group"),
    )
    out_specs = P("group", None, "tensor")
    return jax.shard_map(
        pick, mesh=mesh, in_specs=in_specs, out_specs=out_specs, check_vma=False
    )
```

```python
import jax
import jax.numpy as jnp
import numpy as np
from jax import lax
from jax.experimental import pallas as pl
from jax.experimental.pallas import tpu as pltpu
from jax.sharding import PartitionSpec as P

QUERY_HEADS = 32
KEY_VALUE_HEADS = 4
HEAD_SIZE = 128


rotary_base = 1000000.0


def rotary(heads, positions):
    half = heads.shape[-1] // 2
    expo = jnp.arange(half, dtype=jnp.float32) * 2.0 / heads.shape[-1]
    freqs = rotary_base ** (-expo)
    angles = positions[:, None] * freqs[None, :]
    cosine = jnp.cos(angles)[None]
    sine = jnp.sin(angles)[None]
    first = heads[..., :half]
    second = heads[..., half:]
    return jnp.concatenate(
        [first * cosine - second * sine, second * cosine + first * sine], axis=-1
    )


def per_device(
    turns,
    query_store,
    key_block_holder,
    value_block_holder,
    query_bias,
    key_projection_bias,
    value_projection_bias,
    owner,
    lengths,
):
    tensor_index = lax.axis_index("tensor")
    group_count = lax.axis_size("group")
    gathered = lax.all_gather(turns, "tensor", axis=1, tiled=True)[0]
    token_count = gathered.shape[0]
    block_rows = query_store.shape[1]
    query_cols = query_store.shape[2]
    heads_dev = query_cols // HEAD_SIZE
    query_per_key_head = QUERY_HEADS // KEY_VALUE_HEADS
    key_value_per_group = max(1, heads_dev // query_per_key_head)
    key_value_leading = tensor_index * heads_dev // query_per_key_head
    keys_mine = lax.dynamic_slice_in_dim(
        key_block_holder, key_value_leading, key_value_per_group, 2
    ).reshape(1, block_rows, key_value_per_group * HEAD_SIZE)
    values_mine = lax.dynamic_slice_in_dim(
        value_block_holder, key_value_leading, key_value_per_group, 2
    ).reshape(1, block_rows, key_value_per_group * HEAD_SIZE)
    inverse = (
        jnp.zeros((group_count,), jnp.int32).at[owner].set(jnp.arange(group_count, dtype=jnp.int32))
    )
    ordered = jnp.stack(
        [
            lax.dynamic_slice_in_dim(gathered, inverse[holder] * block_rows, block_rows, 1)
            for holder in range(group_count)
        ],
        axis=1,
    )
    proj_query = jnp.einsum(
        "tgc,gcn->tn",
        ordered,
        lax.all_gather(query_store, "group", axis=0, tiled=True),
        preferred_element_type=jnp.float32,
    )
    proj_key = jnp.einsum(
        "tgc,gcn->tn",
        ordered,
        lax.all_gather(keys_mine, "group", axis=0, tiled=True),
        preferred_element_type=jnp.float32,
    )
    proj_value = jnp.einsum(
        "tgc,gcn->tn",
        ordered,
        lax.all_gather(values_mine, "group", axis=0, tiled=True),
        preferred_element_type=jnp.float32,
    )
    key_bias_rows = lax.dynamic_slice_in_dim(
        key_projection_bias.reshape(KEY_VALUE_HEADS, HEAD_SIZE),
        key_value_leading,
        key_value_per_group,
        0,
    ).reshape(key_value_per_group * HEAD_SIZE)
    bias_values = lax.dynamic_slice_in_dim(
        value_projection_bias.reshape(KEY_VALUE_HEADS, HEAD_SIZE),
        key_value_leading,
        key_value_per_group,
        0,
    ).reshape(key_value_per_group * HEAD_SIZE)
    positions = jnp.arange(token_count, dtype=jnp.float32)
    raw_query = (
        (proj_query + query_bias).reshape(token_count, heads_dev, HEAD_SIZE).transpose(1, 0, 2)
    )
    unbiased_key = (
        (proj_key + key_bias_rows)
        .reshape(token_count, key_value_per_group, HEAD_SIZE)
        .transpose(1, 0, 2)
    )
    unbiased_value = (
        (proj_value + bias_values)
        .reshape(token_count, key_value_per_group, HEAD_SIZE)
        .transpose(1, 0, 2)
    )
    queries = rotary(raw_query, positions).astype(jnp.bfloat16)
    keys_rot = rotary(unbiased_key, positions).astype(jnp.bfloat16)
    values_cast = unbiased_value.astype(jnp.bfloat16)
    repeat_count = heads_dev // key_value_per_group
    keys_full = jnp.repeat(keys_rot, repeat_count, axis=0)
    values_full = jnp.repeat(values_cast, repeat_count, axis=0)
    index = jnp.arange(token_count, dtype=jnp.int32)
    span = min(256, token_count)
    outputs = []
    for block in range(token_count // span):
        first = block * span
        last = first + span
        scores = jnp.einsum(
            "htd,hsd->hts",
            queries[:, first:last],
            keys_full[:, :last],
            preferred_element_type=jnp.float32,
        ) * HEAD_SIZE ** (-0.5)
        causal = index[None, :last] <= index[first:last, None]
        scores = jnp.where(causal[None], scores, -jnp.inf)
        top = jnp.max(scores, axis=-1, keepdims=True)
        expd = jnp.exp(scores - top)
        weights = (expd / jnp.sum(expd, axis=-1, keepdims=True)).astype(jnp.bfloat16)
        outputs.append(
            jnp.einsum(
                "hts,hsd->htd", weights, values_full[:, :last], preferred_element_type=jnp.float32
            )
        )
    mixed = jnp.concatenate(outputs, axis=1)
    mixed = mixed.transpose(1, 0, 2).reshape(token_count, query_cols)
    live = (index < lengths[0])[:, None]
    return jnp.where(live, mixed, 0.0).astype(jnp.bfloat16)[None]


BLOCKS = 16
ROWS = 256
TOKENS = 256
HALF = 128
LAYERS = 4
WIDTHS = (768, 512)
MESH = pl.DeviceIdType.MESH


def plane_kernel(
    row_block_ref,
    length_ref,
    turns_ref,
    store_ref,
    kv_ref,
    query_bias_ref,
    key_bias_ref,
    value_bias_ref,
    cosine_ref,
    sine_ref,
    out_ref,
    x_ref,
    wa_ref,
    wb_ref,
    acca_ref,
    accb_ref,
    keys_ref,
    values_ref,
    back_ref,
    local_sem,
    x_local,
    x_send,
    x_recv,
    y_send,
    y_recv,
    z_send,
    z_recv,
    sib_send,
    sib_recv,
    back_send,
    back_recv,
):
    g = lax.axis_index("group")
    t = lax.axis_index("tensor")
    core = lax.rem(g, 2)
    y = lax.rem(g // 2, 2)
    z = g // 4
    other = 1 - core
    across = g + 2 - 4 * y
    sibling = g + 1 - 2 * core
    weights = (wa_ref, wb_ref)
    accs = (acca_ref, accb_ref)

    def pieces(d):
        first = pl.multiple_of(d * 1024, 1024)
        second = pl.multiple_of(d * 1024 + 512, 512)
        return (
            (kv_ref.at[:, pl.ds(pl.multiple_of(d * 256, 256), 256)], wa_ref.at[core, z, y, :, 0:256]),
            (store_ref.at[0, :, pl.ds(first, 512)], wa_ref.at[core, z, y, :, 256:768]),
            (store_ref.at[0, :, pl.ds(second, 512)], wb_ref.at[core, z, y]),
        )

    loads = [
        pltpu.make_async_copy(source, slot, local_sem.at[i])
        for i, (source, slot) in enumerate(pieces(y))
    ]
    mine = pl.ds(pl.multiple_of((2 * y + t) * HALF, HALF), HALF)
    x_loads = [
        pltpu.make_async_copy(
            turns_ref.at[0, :, b * ROWS : b * ROWS + ROWS], x_ref.at[b, mine], x_local.at[b]
        )
        for b in range(BLOCKS)
    ]
    for load in loads + x_loads:
        load.start()

    barrier = pltpu.get_barrier_semaphore()
    for partner in ((sibling, t), (across, t), (g, 1 - t), (across, 1 - t)):
        pl.semaphore_signal(barrier, inc=1, device_id=partner, device_id_type=MESH)

    @pl.when(z < LAYERS - 1)
    def _():
        pl.semaphore_signal(barrier, inc=1, device_id=(g + 4, t), device_id_type=MESH)

    @pl.when(z > 0)
    def _():
        pl.semaphore_signal(barrier, inc=1, device_id=(g - 4, t), device_id_type=MESH)

    pl.semaphore_wait(barrier, 4 + (z + 2) // 3 + (5 - z) // 3)

    def remote(source, slot, send, recv, device):
        return pltpu.make_async_remote_copy(
            src_ref=source,
            dst_ref=slot,
            send_sem=send,
            recv_sem=recv,
            device_id=device,
            device_id_type=MESH,
        )

    y_copies = [
        remote(source, slot, y_send.at[i], y_recv.at[i], (across, t))
        for i, (source, slot) in enumerate(pieces(1 - y))
    ]

    def y_arrival(i):
        slot = (wa_ref.at[core, z, 1 - y, :, 0:256], wa_ref.at[core, z, 1 - y, :, 256:768],
                wb_ref.at[core, z, 1 - y])[i]
        return remote(slot, slot, y_send.at[i], y_recv.at[i], (across, t))

    def row_of(h):
        return y if h == 0 else 1 - y

    def origin(d, k):
        return z - 1 - k if d == 0 else z + 1 + k

    def arrives(d, k):
        return z - 1 - k >= 0 if d == 0 else z + 1 + k < LAYERS

    def goes_on(d):
        return z < LAYERS - 1 if d == 0 else z > 0

    def z_copy(u, d, k, h):
        slot = weights[u].at[core, origin(d, k - 1), row_of(h)]
        device = (g + 4, t) if d == 0 else (g - 4, t)
        return remote(slot, slot, z_send.at[u, d, k, h], z_recv.at[u, d, k, h], device)

    def z_arrival(u, d, k, h):
        slot = weights[u].at[core, origin(d, k), row_of(h)]
        device = (g + 4, t) if d == 0 else (g - 4, t)
        return remote(slot, slot, z_send.at[u, d, k, h], z_recv.at[u, d, k, h], device)

    def sib_copy(u, d, k, h, which):
        slot = weights[u].at[which, origin(d, k), row_of(h)]
        j = 0 if k < 0 else 1 + 2 * k + d
        return remote(slot, slot, sib_send.at[u, j, h], sib_recv.at[u, j, h], (sibling, t))

    def send_home(u, h):
        for d in range(2):

            @pl.when(goes_on(d))
            def _():
                z_copy(u, d, 0, h).start()

        sib_copy(u, 0, -1, h, core).start()

    x_targets = ((g, 1 - t), (across, t), (across, 1 - t))
    x_copies = [
        remote(x_ref.at[:, mine], x_ref.at[:, mine], x_send.at[i], x_recv.at[i], device)
        for i, device in enumerate(x_targets)
    ]

    def x_arrival(i):
        spot = ((2 * y + 1 - t), (2 * (1 - y) + t), (2 * (1 - y) + 1 - t))[i]
        rows = x_ref.at[:, pl.ds(pl.multiple_of(spot * HALF, HALF), HALF)]
        return remote(rows, rows, x_send.at[i], x_recv.at[i], x_targets[i])

    y_copies[0].start()
    y_copies[1].start()
    loads[0].wait()
    loads[1].wait()
    send_home(0, 0)
    y_copies[2].start()
    for load in x_loads:
        load.wait()
    for copy in x_copies:
        copy.start()
    loads[2].wait()
    send_home(1, 0)

    head = pl.ds(pl.multiple_of((2 * t + y) * HEAD_SIZE, HEAD_SIZE), HEAD_SIZE)
    first = pl.ds(pl.multiple_of(y * 1024, 1024), 512)
    second = pl.ds(pl.multiple_of(y * 1024 + 512, 512), 512)
    acca_ref[:, 0:128] = jnp.broadcast_to(key_bias_ref[:, head], (2 * TOKENS, 128))
    acca_ref[:, 128:256] = jnp.broadcast_to(value_bias_ref[:, head], (2 * TOKENS, 128))
    acca_ref[:, 256:768] = jnp.broadcast_to(query_bias_ref[:, first], (2 * TOKENS, 512))
    accb_ref[...] = jnp.broadcast_to(query_bias_ref[:, second], (2 * TOKENS, 512))

    y_arrival(0).wait_recv()
    y_arrival(1).wait_recv()
    send_home(0, 1)
    y_arrival(2).wait_recv()
    send_home(1, 1)

    def forward(u, k):
        for h in range(2):
            for d in range(2):

                @pl.when(arrives(d, k))
                def _():
                    z_arrival(u, d, k, h).wait_recv()
                    if k < LAYERS - 2:

                        @pl.when(goes_on(d))
                        def _():
                            z_copy(u, d, k + 1, h).start()

                    sib_copy(u, d, k, h, core).start()

    def add_product(u, layer, row, which):
        holder = layer * 4 + row * 2 + which
        accs[u][...] += jnp.dot(
            x_ref[row_block_ref[holder]],
            weights[u][which, layer, row],
            preferred_element_type=jnp.float32,
        )

    def use(u, k):
        def both(layer):
            def body(i, carry):
                add_product(u, layer, i // 2, lax.rem(i, 2))
                return carry

            lax.fori_loop(0, 4, body, 0)

        if k < 0:
            for h in range(2):
                sib_copy(u, 0, -1, h, other).wait_recv()
            both(z)
            return
        for d in range(2):

            @pl.when(arrives(d, k))
            def _():
                for h in range(2):
                    sib_copy(u, d, k, h, other).wait_recv()
                both(origin(d, k))

    def rotate(raw):
        return (raw * cosine_ref[...] + pltpu.roll(raw, 64, 1) * sine_ref[...]).astype(jnp.bfloat16)

    scale = HEAD_SIZE ** (-0.5)

    def rows_of(side):
        return pl.ds(pl.multiple_of(side * TOKENS, TOKENS), TOKENS)

    def attend(raw, side):
        query = rotate(raw)
        parts = []
        for piece in range(2):
            low, high = piece * HALF, piece * HALF + HALF
            scores = (
                lax.dot_general(
                    query[low:high],
                    keys_ref[side, 0:high],
                    (((1,), (1,)), ((), ())),
                    preferred_element_type=jnp.float32,
                )
                * scale
            )
            rows = lax.broadcasted_iota(jnp.int32, (HALF, high), 0) + low
            cols = lax.broadcasted_iota(jnp.int32, (HALF, high), 1)
            scores = jnp.where(cols <= rows, scores, -jnp.inf)
            top = jnp.max(scores, axis=-1, keepdims=True)
            expd = jnp.exp(scores - top)
            total = jnp.sum(expd, axis=-1, keepdims=True)
            shares = (expd / total).astype(jnp.bfloat16)
            parts.append(
                jnp.dot(shares, values_ref[side, 0:high], preferred_element_type=jnp.float32)
            )
        return parts

    def back_copy(u, p):
        to = pl.ds(pl.multiple_of(y * 1024 + u * 512 + p * 256, 256), 256)
        return remote(
            back_ref.at[u, p], out_ref.at[0, :, to], back_send.at[u, p], back_recv.at[u, p], (across, t)
        )

    def back_arrival(u, p):
        to = pl.ds(pl.multiple_of((1 - y) * 1024 + u * 512 + p * 256, 256), 256)
        return remote(
            back_ref.at[u, p], out_ref.at[0, :, to], back_send.at[u, p], back_recv.at[u, p], (across, t)
        )

    length = length_ref[0]

    def attention(u):
        start = 256 if u == 0 else 0
        for p in range(2):
            for e in range(2):
                lane = start + p * 256 + e * HEAD_SIZE
                parts = attend(accs[u][rows_of(1 - y), lane : lane + HEAD_SIZE], 1 - y)
                for piece in range(2):
                    back_ref[
                        u, p, piece * HALF : piece * HALF + HALF, e * HEAD_SIZE : e * HEAD_SIZE + HEAD_SIZE
                    ] = parts[piece].astype(jnp.bfloat16)
            back_copy(u, p).start()
        for e in range(4):
            lane = start + e * HEAD_SIZE
            parts = attend(accs[u][rows_of(y), lane : lane + HEAD_SIZE], y)
            to = pl.ds(pl.multiple_of(y * 1024 + u * 512 + e * HEAD_SIZE, HEAD_SIZE), HEAD_SIZE)
            for piece in range(2):
                live = lax.broadcasted_iota(jnp.int32, (HALF, HEAD_SIZE), 0) + piece * HALF < length
                out_ref[0, piece * HALF : piece * HALF + HALF, to] = jnp.where(
                    live, parts[piece], 0.0
                ).astype(jnp.bfloat16)

    forward(0, 0)
    forward(0, 1)
    forward(1, 0)
    for i in range(3):
        x_arrival(i).wait_recv()
    use(0, -1)
    use(0, 0)
    forward(0, 2)
    use(0, 1)
    forward(1, 1)
    use(0, 2)
    for side in range(2):
        rows = slice(side * TOKENS, side * TOKENS + TOKENS)
        keys_ref[side] = rotate(acca_ref[rows, 0:128])
        values_ref[side] = acca_ref[rows, 128:256].astype(jnp.bfloat16)
    attention(0)
    use(1, -1)
    use(1, 0)
    use(1, 1)
    forward(1, 2)
    use(1, 2)
    attention(1)

    for u in range(2):
        for p in range(2):
            back_arrival(u, p).wait_recv()
            to = pl.ds(pl.multiple_of((1 - y) * 1024 + u * 512 + p * 256, 256), 256)
            live = lax.broadcasted_iota(jnp.int32, (TOKENS, 256), 0) < length
            got = out_ref[0, :, to].astype(jnp.float32)
            out_ref[0, :, to] = jnp.where(live, got, 0.0).astype(jnp.bfloat16)

    for i in range(3):
        y_copies[i].wait_send()
        x_copies[i].wait_send()
    for u in range(2):
        for h in range(2):
            back_copy(u, h).wait_send()
            sib_copy(u, 0, -1, h, core).wait_send()
            for d in range(2):

                @pl.when(goes_on(d))
                def _():
                    z_copy(u, d, 0, h).wait_send()

                for k in range(LAYERS - 1):

                    @pl.when(arrives(d, k))
                    def _():
                        sib_copy(u, d, k, h, core).wait_send()
                        if k < LAYERS - 2:

                            @pl.when(goes_on(d))
                            def _():
                                z_copy(u, d, k + 1, h).wait_send()


def rotary_tables():
    freqs = rotary_base ** (-2.0 * np.arange(64) / HEAD_SIZE)
    angles = np.arange(TOKENS)[:, None] * freqs[None, :]
    cosine, sine = np.cos(angles), np.sin(angles)
    return (
        np.concatenate([cosine, cosine], axis=1).astype(np.float32),
        np.concatenate([-sine, sine], axis=1).astype(np.float32),
    )


def per_device_plane(
    turns,
    query_store,
    key_block_holder,
    value_block_holder,
    query_bias,
    key_projection_bias,
    value_projection_bias,
    owner,
    lengths,
):
    t = lax.axis_index("tensor")
    keys_mine = lax.dynamic_slice_in_dim(key_block_holder[0], 2 * t, 2, 1)
    values_mine = lax.dynamic_slice_in_dim(value_block_holder[0], 2 * t, 2, 1)
    kv = jnp.concatenate([keys_mine, values_mine], axis=2).reshape(ROWS, 512)
    numbers = jnp.arange(BLOCKS, dtype=jnp.int32)
    row_block = jnp.sum(
        jnp.where(owner[None, :] == numbers[:, None], numbers[None, :], 0), axis=1, dtype=jnp.int32
    )
    cosine, sine = rotary_tables()
    smem = pl.BlockSpec(memory_space=pltpu.SMEM)
    vmem = pl.BlockSpec(memory_space=pltpu.VMEM)
    hbm = pl.BlockSpec(memory_space=pl.ANY)
    return pl.pallas_call(
        plane_kernel,
        out_shape=jax.ShapeDtypeStruct((1, TOKENS, 2048), jnp.bfloat16),
        in_specs=[smem, smem, hbm, hbm, hbm, vmem, vmem, vmem, vmem, vmem],
        out_specs=vmem,
        scratch_shapes=[
            pltpu.VMEM((BLOCKS, 2 * TOKENS, ROWS), jnp.bfloat16),
            pltpu.VMEM((2, LAYERS, 2, ROWS, WIDTHS[0]), jnp.bfloat16),
            pltpu.VMEM((2, LAYERS, 2, ROWS, WIDTHS[1]), jnp.bfloat16),
            pltpu.VMEM((2 * TOKENS, WIDTHS[0]), jnp.float32),
            pltpu.VMEM((2 * TOKENS, WIDTHS[1]), jnp.float32),
            pltpu.VMEM((2, TOKENS, HEAD_SIZE), jnp.bfloat16),
            pltpu.VMEM((2, TOKENS, HEAD_SIZE), jnp.bfloat16),
            pltpu.VMEM((2, 2, TOKENS, 256), jnp.bfloat16),
            pltpu.SemaphoreType.DMA((3,)),
            pltpu.SemaphoreType.DMA((BLOCKS,)),
            pltpu.SemaphoreType.DMA((3,)),
            pltpu.SemaphoreType.DMA((3,)),
            pltpu.SemaphoreType.DMA((3,)),
            pltpu.SemaphoreType.DMA((3,)),
            pltpu.SemaphoreType.DMA((2, 2, LAYERS - 1, 2)),
            pltpu.SemaphoreType.DMA((2, 2, LAYERS - 1, 2)),
            pltpu.SemaphoreType.DMA((2, 7, 2)),
            pltpu.SemaphoreType.DMA((2, 7, 2)),
            pltpu.SemaphoreType.DMA((2, 2)),
            pltpu.SemaphoreType.DMA((2, 2)),
        ],
        compiler_params=pltpu.CompilerParams(
            collective_id=0, has_side_effects=True, vmem_limit_bytes=48 * 1024 * 1024
        ),
    )(
        row_block,
        lengths,
        turns,
        query_store,
        kv,
        query_bias[None],
        key_projection_bias[None],
        value_projection_bias[None],
        jnp.asarray(cosine),
        jnp.asarray(sine),
    )


def pick(turns, *rest):
    fits = lax.axis_size("group") == 16 and lax.axis_size("tensor") == 2
    fits = fits and turns.shape[1:] == (128, 4096)
    return per_device_plane(turns, *rest) if fits else per_device(turns, *rest)


def solution(mesh):
    in_specs = (
        P("group", "tensor", None),
        P("group", None, "tensor"),
        P("group", None, None, None),
        P("group", None, None, None),
        P("tensor"),
        P(),
        P(),
        P(),
        P("group"),
    )
    out_specs = P("group", None, "tensor")
    return jax.shard_map(
        pick, mesh=mesh, in_specs=in_specs, out_specs=out_specs, check_vma=False
    )
```
